32 devices in a mesh: dp: 4 (over x, core), tensor: 8 (over z, y).
Axes of the slice: x: 2, y: 2, z: 4, core: 2. Of those that a mesh axis runs over, the one named last changes fastest.
Arguments:
- activations: bfloat16 [512, 29696], P('dp', 'tensor'), may hold values from -6 to 6
- weight_codes: bfloat16 [29696, 7424], P('tensor'), may hold values from -127 to 127, as said below
- channel_scale: float32 [7424], replicated, may hold values from 0.0006565322 to 0.0065653217
- output_grads: bfloat16 [512, 7424], P('dp', 'tensor'), may hold values from -0.375 to 0.375
Outputs:
- input_grads: float32 [512, 29696], P('dp', 'tensor')
- weight_grads: float32 [29696, 7424], P('tensor', 'dp')
The draws below stay inside these ranges and needn't reach their ends.
Inputs may be any that keep to these rules, and one draw needn't show every extreme that they name: weight_codes holds whole numbers.
All inputs are finite; a program needn't handle non-finite values.
Results may differ from the reference program's by a relative error of at most 0.0029.
Values may be sent and summed in bfloat16 or wider, within the bound.
A program may use at most 128 MiB of HBM per device.

```python
import math
import jax
import jax.numpy as jnp

D = 7424
FF = 29696
TOKENS = 512


def draw_weight_codes(key, part):
    key = jax.random.fold_in(key, 7)
    values = jax.random.randint(key, (FF, D), -127, 128)
    return values.astype(jnp.float32).astype(jnp.bfloat16)


def strengthened(values, key, source, target, blocks, factor):
    owner, partner = [(jnp.arange(values.shape[position]) // (values.shape[position] // blocks)).reshape([-1 if axis == position else 1 for axis in range(values.ndim)]) for position in (source, target)]
    chosen = jax.random.permutation(key, blocks)[partner]
    strong = (owner == chosen) | (owner == (partner + blocks // 2) % blocks)
    return jnp.where(strong, factor * values, values)


def shard_levels(stream_key, extent, split, least, top_value):
    def one(dim, blocks):
        heights = jax.random.uniform(jax.random.fold_in(jax.random.fold_in(stream_key, 6), dim), (blocks,), jnp.float32, least / len(split), top_value / len(split))
        return jnp.repeat(jnp.exp(heights), extent[dim] // blocks).reshape((-1,) + (1,) * (len(extent) - dim - 1))

    loudness = one(*split[0])
    for cut in split[1:]:
        loudness = loudness * one(*cut)
    return loudness


def bell_draw(rng, extent, scale, most, shards=(), held_as=jnp.bfloat16):
    array = jax.random.normal(rng, extent, jnp.float32) * scale
    if len(shards) > 0:
        array = shard_levels(rng, extent, shards, -0.22, 0.18) * array
    return jnp.clip(array, min=-most, max=most).astype(held_as)


def gaussian_with(key, dims, deviation, most, shards, heavy, kind=jnp.bfloat16):
    entries = deviation * jax.random.normal(key, dims, jnp.float32)
    if shards:
        entries = entries * shard_levels(key, dims, shards, -0.22, 0.18)
    return jnp.clip(strengthened(entries, jax.random.fold_in(key, 3), *heavy), -most, most).astype(kind)


def setup_inputs(seed: int = 0) -> dict:
    keys = jax.random.split(jax.random.key(seed), 5)
    return {
        "activations": bell_draw(keys[0], (TOKENS, FF), 1.0, 6.0, ((0, 4), (1, 8))),
        "weight_codes": draw_weight_codes(jax.random.fold_in(keys[4], 71), 0),
        "channel_scale": jnp.clip(jnp.exp(jax.random.uniform(keys[2], (D,), jnp.float32, math.log(0.0006565322), math.log(0.0065653217))), 0.0006565322, 0.0065653217),
        "output_grads": gaussian_with(keys[3], (TOKENS, D), (1 / TOKENS ** 0.5), 0.375, ((0, 4), (1, 8)), (0, 1, 8, 2.0)),
    }


def reference(activations, weight_codes, channel_scale, output_grads):
    scaled = (output_grads.astype(jnp.float32) * channel_scale).astype(jnp.bfloat16)
    input_grads = jnp.dot(scaled, weight_codes.T, preferred_element_type=jnp.float32)
    weight_grads = jnp.dot(activations.T, output_grads, preferred_element_type=jnp.float32)
    return input_grads, weight_grads
```

```python
import functools

import jax
import jax.numpy as jnp
from jax import lax
from jax.experimental import pallas as pl
from jax.experimental.pallas import tpu as pltpu
from jax.sharding import PartitionSpec as P

MESH = pl.DeviceIdType.MESH
BF16, F32 = jnp.bfloat16, jnp.float32
LINE = 4
LANES = 128


def gather_kernel(
    a_ref, g_ref, s_ref, w_ref, ig_ref, at_ref, og_ref,
    codes, gbuf, cross, gs, scale, acc, ig_own, ig_sib,
    code_sem, up_sem, down_sem, y_sem, sib_sem, line_recv, y_recv, sib_recv,
    cross_sem, cup_sem, cdown_sem, cy_sem, cross_recv, cy_recv,
    ax_sem, as_sem, ax_recv, as_recv, al_sem, og_sem, ig_sem, g_sem,
):
    dp, j = lax.axis_index("dp"), lax.axis_index("tensor")
    x, c = lax.div(dp, 2), lax.rem(dp, 2)
    z, y = lax.div(j, 2), lax.rem(j, 2)
    hidden = a_ref.shape[1]
    channels = g_ref.shape[0]
    depth = w_ref.shape[1]
    rows = codes.shape[0]
    step_rows = hidden - rows
    half = depth // 2
    sibling = (2 * x + 1 - c, j)
    across = (2 * (1 - x) + c, j)
    beside = (dp, 2 * z + 1 - y)
    above = (dp, j + 2)
    below = (dp, j - 2)

    def code_copy(i):
        n = rows // 5
        return pltpu.make_async_copy(
            w_ref.at[pl.ds(pl.multiple_of(c * step_rows + i * n, 128), n)],
            codes.at[pl.ds(i * n, n)], code_sem.at[i])

    for i in range(5):
        code_copy(i).start()

    barrier = pltpu.get_barrier_semaphore()

    def greet(device):
        pl.semaphore_signal(barrier, inc=1, device_id=device, device_id_type=MESH)

    greet(sibling)
    greet(beside)
    greet((2 * (1 - x), j))
    greet((2 * (1 - x) + 1, j))

    @pl.when(z < LINE - 1)
    def _():
        greet(above)

    @pl.when(z > 0)
    def _():
        greet(below)

    g_local = pltpu.make_async_copy(
        g_ref, gbuf.at[c, pl.ds(pl.multiple_of(j * channels, 32), channels)], g_sem.at[0])
    g_local.start()

    ends = jnp.logical_or(z == 0, z == LINE - 1)
    pl.semaphore_wait(barrier, jnp.where(ends, 5, 6))

    def remote(src, dst, send, recv, device):
        return pltpu.make_async_remote_copy(
            src_ref=src, dst_ref=dst, send_sem=send, recv_sem=recv,
            device_id=device, device_id_type=MESH)

    def slot(core, zz, yy):
        start = pl.multiple_of((2 * zz + yy) * channels, 32)
        return gbuf.at[core, pl.ds(start, channels)]

    def up(zz, src=None):
        s = slot(c, zz, y)
        return remote(s if src is None else src, s, up_sem.at[zz], line_recv.at[zz], above)

    def down(zz, src=None):
        s = slot(c, zz, y)
        return remote(s if src is None else src, s, down_sem.at[zz], line_recv.at[zz], below)

    def side(zz, src=None):
        s = slot(c, zz, y)
        return remote(s if src is None else src, s, y_sem.at[zz], y_recv.at[zz], beside)

    def from_side(zz):
        s = slot(c, zz, 1 - y)
        return remote(s, s, y_sem.at[zz], y_recv.at[zz], beside)

    def to_sib(zz, yy, src=None):
        s = slot(c, zz, yy)
        k = 2 * zz + yy
        return remote(s if src is None else src, s, sib_sem.at[k], sib_recv.at[k], sibling)

    def from_sib(zz, yy):
        s = slot(1 - c, zz, yy)
        k = 2 * zz + yy
        return remote(s, s, sib_sem.at[k], sib_recv.at[k], sibling)

    entry = 2 * x + c
    away = jnp.abs(z - entry)
    sends_cross = lax.div(z, 2) != x

    def cross_out():
        return remote(g_ref, cross.at[c, y], cross_sem.at[0], cross_recv.at[c],
                      (2 * (1 - x) + lax.rem(z, 2), j))

    def cross_move(k, send, recv, device):
        return remote(cross.at[k, y], cross.at[k, y], send.at[k], recv.at[k], device)

    def cross_up(k):
        return cross_move(k, cup_sem, cross_recv, above)

    def cross_down(k):
        return cross_move(k, cdown_sem, cross_recv, below)

    def cross_side(k):
        return cross_move(k, cy_sem, cy_recv, beside)

    def cross_from_side(k):
        return remote(cross.at[k, 1 - y], cross.at[k, 1 - y], cy_sem.at[k], cy_recv.at[k], beside)

    goes_up = jnp.logical_and(z >= entry, z < LINE - 1)
    goes_down = jnp.logical_and(z <= entry, z > 0)

    @pl.when(sends_cross)
    def _():
        cross_out().start()

    @pl.when(z < LINE - 1)
    def _():
        up(z, g_ref).start()

    @pl.when(z > 0)
    def _():
        down(z, g_ref).start()

    side(z, g_ref).start()
    to_sib(z, y, g_ref).start()

    piece = a_ref.shape[0] // 4

    def acts(i, index):
        start = pl.multiple_of(index * a_ref.shape[0] + i * piece, piece)
        return at_ref.at[pl.ds(start, piece)]

    def own_acts(i):
        return a_ref.at[pl.ds(i * piece, piece)]

    def acts_across(i):
        return remote(own_acts(i), acts(i, dp), ax_sem.at[i], ax_recv.at[i], across)

    def acts_from_across(i):
        s = acts(i, 2 * (1 - x) + c)
        return remote(s, s, ax_sem.at[i], ax_recv.at[i], across)

    def acts_sib(i):
        return remote(own_acts(i), acts(i, dp), as_sem.at[i], as_recv.at[i], sibling)

    def acts_from_sib(i):
        s = acts(i, 2 * x + 1 - c)
        return remote(s, s, as_sem.at[i], as_recv.at[i], sibling)

    def acts_on(i):
        s = acts(i, 2 * (1 - x) + c)
        return remote(s, s, as_sem.at[4 + i], as_recv.at[4 + i], sibling)

    def acts_on_from(i):
        s = acts(i, 2 * (1 - x) + 1 - c)
        return remote(s, s, as_sem.at[4 + i], as_recv.at[4 + i], sibling)

    def acts_local(i):
        return pltpu.make_async_copy(own_acts(i), acts(i, dp), al_sem.at[i])

    for i in range(4):
        acts_across(i).start()
    for i in range(4):
        acts_sib(i).start()
        acts_local(i).start()

    @pl.loop(0, depth // LANES)
    def _(t):
        r = pl.ds(pl.multiple_of(t * LANES, LANES), LANES)
        scale[r, :] = jnp.broadcast_to(s_ref[r][None, :], (LANES, LANES)).T

    def relay_cross():
        for k in range(2):
            cross_up(k).wait_recv()

            @pl.when(goes_up)
            def _():
                cross_up(k).start()

            @pl.when(goes_down)
            def _():
                cross_down(k).start()

            cross_side(k).start()

    def pass_side(d):
        def one(zz):
            from_side(zz).wait_recv()
            to_sib(zz, 1 - y).start()

        if d == 0:
            one(z)
        else:
            pl.when(z - d >= 0)(lambda: one(z - d))
            pl.when(z + d <= LINE - 1)(lambda: one(z + d))

    for d in range(1, LINE):
        @pl.when(z - d >= 0)
        def _():
            zz = z - d
            up(zz).wait_recv()

            @pl.when(z < LINE - 1)
            def _():
                up(zz).start()

            side(zz).start()
            to_sib(zz, y).start()

        @pl.when(z + d <= LINE - 1)
        def _():
            zz = z + d
            down(zz).wait_recv()

            @pl.when(z > 0)
            def _():
                down(zz).start()

            side(zz).start()
            to_sib(zz, y).start()

        pl.when(away == d - 1)(relay_cross)
        if d >= 2:
            pass_side(d - 2)

    g_local.wait()
    for i in range(5):
        code_copy(i).wait()

    def multiply(h, first):
        for zz in range(2):
            for yy in range(2):
                from_sib(2 * h + zz, yy).wait_recv()
        base = h * half

        @pl.loop(0, half // LANES)
        def _(t):
            r = pl.ds(pl.multiple_of(base + t * LANES, LANES), LANES)
            q = pl.ds(pl.multiple_of(t * LANES, LANES), LANES)
            by = scale[r, :]
            gs[q, :LANES] = (gbuf[0, r, :].astype(F32) * by).astype(BF16)
            gs[q, LANES:] = (gbuf[1, r, :].astype(F32) * by).astype(BF16)

        tile = rows // 5

        @pl.loop(0, 5)
        def _(t):
            r = pl.ds(pl.multiple_of(t * tile, tile), tile)
            k = pl.ds(pl.multiple_of(base, LANES), half)
            part = jnp.dot(codes[r, k], gs[...], preferred_element_type=F32)
            acc[r, :] = part if first else acc[r, :] + part

    near = lax.div(z, 2)
    multiply(near, True)
    pl.when(away == LINE - 1)(relay_cross)
    pass_side(LINE - 2)
    pass_side(LINE - 1)
    for i in range(2):
        acts_from_across(i).wait_recv()
        acts_on(i).start()
    multiply(1 - near, False)

    @pl.loop(0, rows // LANES)
    def _(t):
        r = pl.ds(pl.multiple_of(t * LANES, LANES), LANES)
        ig_sib[:, r] = acc[r, pl.ds(pl.multiple_of((1 - c) * LANES, LANES), LANES)].T
        ig_own[:, r] = acc[r, pl.ds(pl.multiple_of(c * LANES, LANES), LANES)].T

    def ig_out():
        return remote(
            ig_sib.at[:, pl.ds(pl.multiple_of(c * (rows - step_rows), LANES), step_rows)],
            ig_ref.at[:, pl.ds(pl.multiple_of(c * rows, LANES), step_rows)],
            ig_sem.at[0], ig_sem.at[1], sibling)

    def ig_in():
        s = ig_ref.at[:, pl.ds(pl.multiple_of((1 - c) * rows, LANES), step_rows)]
        return remote(s, s, ig_sem.at[0], ig_sem.at[1], sibling)

    ig_local = pltpu.make_async_copy(
        ig_own, ig_ref.at[:, pl.ds(pl.multiple_of(c * step_rows, LANES), rows)], ig_sem.at[2])
    ig_out().start()
    ig_local.start()

    for i in range(2, 4):
        acts_from_across(i).wait_recv()
        acts_on(i).start()

    block = pl.ds(pl.multiple_of(2 * entry * channels, 32), 2 * channels)
    og_copies = [
        pltpu.make_async_copy(gbuf.at[k, block], og_ref.at[2 * x + k], og_sem.at[k])
        for k in range(2)
    ]
    for k in range(2):
        og_copies[k].start()
    for k in range(2):
        cross_from_side(k).wait_recv()
        for yy in range(2):
            og_copies.append(pltpu.make_async_copy(
                cross.at[k, yy], og_ref.at[2 * (1 - x) + k, pl.ds(yy * channels, channels)],
                og_sem.at[2 + 2 * k + yy]))
            og_copies[-1].start()

    for zz in range(LINE):
        @pl.when(jnp.logical_and(zz <= z, z < LINE - 1))
        def _():
            up(zz).wait_send()

        @pl.when(jnp.logical_and(zz >= z, z > 0))
        def _():
            down(zz).wait_send()

        side(zz).wait_send()
        for yy in range(2):
            to_sib(zz, yy).wait_send()

    @pl.when(sends_cross)
    def _():
        cross_out().wait_send()

    for k in range(2):
        @pl.when(goes_up)
        def _():
            cross_up(k).wait_send()

        @pl.when(goes_down)
        def _():
            cross_down(k).wait_send()

        cross_side(k).wait_send()

    for i in range(4):
        acts_across(i).wait_send()
        acts_sib(i).wait_send()
        acts_on(i).wait_send()
        acts_local(i).wait()
        acts_from_sib(i).wait_recv()
        acts_on_from(i).wait_recv()
    for copy in og_copies:
        copy.wait()
    ig_local.wait()
    ig_out().wait_send()
    ig_in().wait_recv()


def weight_kernel(o_ref, a_ref, out_ref):
    o = jnp.concatenate([o_ref[k] for k in range(4)], axis=1)
    out_ref[...] = jnp.dot(o, a_ref[...], preferred_element_type=F32)


def per_device_kernels(activations, weight_codes, channel_scale, output_grads):
    tokens, hidden = activations.shape
    channels = output_grads.shape[1]
    depth = weight_codes.shape[1]
    rows = (hidden // LANES + 1) // 2 * LANES
    dma = pltpu.SemaphoreType.DMA
    vmem = pl.BlockSpec(memory_space=pltpu.VMEM)
    anywhere = pl.BlockSpec(memory_space=pl.ANY)
    input_grads, acts, grads = pl.pallas_call(
        gather_kernel,
        out_shape=(
            jax.ShapeDtypeStruct((tokens, hidden), F32),
            jax.ShapeDtypeStruct((4 * tokens, hidden), BF16),
            jax.ShapeDtypeStruct((4, 2 * channels, tokens), BF16),
        ),
        in_specs=[anywhere, anywhere, vmem, anywhere],
        out_specs=(anywhere,) * 3,
        scratch_shapes=[
            pltpu.VMEM((rows, depth), BF16),
            pltpu.VMEM((2, depth, tokens), BF16),
            pltpu.VMEM((2, 2, channels, tokens), BF16),
            pltpu.VMEM((depth // 2, 2 * tokens), BF16),
            pltpu.VMEM((depth, LANES), F32),
            pltpu.VMEM((rows, 2 * tokens), F32),
            pltpu.VMEM((tokens, rows), F32),
            pltpu.VMEM((tokens, rows), F32),
            dma((5,)), dma((4,)), dma((4,)), dma((4,)), dma((8,)), dma((4,)), dma((4,)), dma((8,)),
            dma((1,)), dma((2,)), dma((2,)), dma((2,)), dma((2,)), dma((2,)),
            dma((4,)), dma((8,)), dma((4,)), dma((8,)), dma((4,)), dma((6,)), dma((3,)), dma((1,)),
        ],
        compiler_params=pltpu.CompilerParams(
            collective_id=0, has_side_effects=True, vmem_limit_bytes=56 * 2**20),
    )(activations, output_grads.T, channel_scale, weight_codes)
    tile = 256
    weight_grads = pl.pallas_call(
        weight_kernel,
        grid=(pl.cdiv(2 * channels, tile),),
        out_shape=jax.ShapeDtypeStruct((2 * channels, hidden), F32),
        in_specs=[
            pl.BlockSpec((4, tile, tokens), lambda i: (0, i, 0)),
            pl.BlockSpec((4 * tokens, hidden), lambda i: (0, 0)),
        ],
        out_specs=pl.BlockSpec((tile, hidden), lambda i: (i, 0)),
        compiler_params=pltpu.CompilerParams(vmem_limit_bytes=40 * 2**20),
    )(grads, acts)
    return input_grads, weight_grads.T


def per_device_plain(activations, weight_codes, channel_scale, output_grads):
    full_rows = lax.all_gather(output_grads, "tensor", axis=1, tiled=True)
    scaled = (full_rows.astype(F32) * channel_scale).astype(BF16)
    input_grads = lax.dot_general(
        scaled, weight_codes, (((1,), (1,)), ((), ())), preferred_element_type=F32)
    grad_columns = lax.all_to_all(full_rows, "dp", split_axis=1, concat_axis=0, tiled=True)
    weight_grads = lax.dot_general(
        lax.all_gather(activations, "dp", axis=0, tiled=True), grad_columns,
        (((0,), (0,)), ((), ())), preferred_element_type=F32)
    return input_grads, weight_grads


def solution(mesh):
    placed = (P("dp", "tensor"), P("tensor", None), P(), P("dp", "tensor"))
    small = mesh.shape["dp"] == 4 and mesh.shape["tensor"] == 2 * LINE

    return jax.shard_map(
        per_device_kernels if small else per_device_plain,
        mesh=mesh,
        in_specs=placed,
        out_specs=(P("dp", "tensor"), P("tensor", "dp")),
        check_vma=False,
    )
```

```python
import functools

import jax
import jax.numpy as jnp
from jax import lax
from jax.experimental import pallas as pl
from jax.experimental.pallas import tpu as pltpu
from jax.sharding import PartitionSpec as P

MESH = pl.DeviceIdType.MESH
BF16, F32 = jnp.bfloat16, jnp.float32
LINE = 4
LANES = 128


def gather_kernel(
    a_ref, g_ref, s_ref, w_ref, ig_ref, at_ref, og_ref,
    codes, gbuf, cross, gs, acc,
    code_sem, up_sem, down_sem, y_sem, sib_sem, line_recv, y_recv, sib_recv,
    cross_sem, cup_sem, cdown_sem, cy_sem, cross_recv, cy_recv,
    ax_sem, as_sem, ax_recv, as_recv, al_sem, og_sem, ig_sem, g_sem,
):
    dp, j = lax.axis_index("dp"), lax.axis_index("tensor")
    x, c = lax.div(dp, 2), lax.rem(dp, 2)
    z, y = lax.div(j, 2), lax.rem(j, 2)
    hidden = a_ref.shape[1]
    channels = g_ref.shape[0]
    depth = w_ref.shape[1]
    rows = codes.shape[0]
    step_rows = hidden - rows
    half = depth // 2
    sibling = (2 * x + 1 - c, j)
    across = (2 * (1 - x) + c, j)
    beside = (dp, 2 * z + 1 - y)
    above = (dp, j + 2)
    below = (dp, j - 2)

    def code_copy(i):
        n = rows // 5
        return pltpu.make_async_copy(
            w_ref.at[pl.ds(pl.multiple_of(c * step_rows + i * n, 128), n)],
            codes.at[pl.ds(i * n, n)], code_sem.at[i])

    for i in range(5):
        code_copy(i).start()

    barrier = pltpu.get_barrier_semaphore()

    def greet(device):
        pl.semaphore_signal(barrier, inc=1, device_id=device, device_id_type=MESH)

    greet(sibling)
    greet(beside)
    greet((2 * (1 - x), j))
    greet((2 * (1 - x) + 1, j))

    @pl.when(z < LINE - 1)
    def _():
        greet(above)

    @pl.when(z > 0)
    def _():
        greet(below)

    g_local = pltpu.make_async_copy(
        g_ref, gbuf.at[c, pl.ds(pl.multiple_of(j * channels, 32), channels)], g_sem.at[0])
    g_local.start()

    ends = jnp.logical_or(z == 0, z == LINE - 1)
    pl.semaphore_wait(barrier, jnp.where(ends, 5, 6))

    def remote(src, dst, send, recv, device):
        return pltpu.make_async_remote_copy(
            src_ref=src, dst_ref=dst, send_sem=send, recv_sem=recv,
            device_id=device, device_id_type=MESH)

    def slot(core, zz, yy):
        start = pl.multiple_of((2 * zz + yy) * channels, 32)
        return gbuf.at[core, pl.ds(start, channels)]

    def up(zz, src=None):
        s = slot(c, zz, y)
        return remote(s if src is None else src, s, up_sem.at[zz], line_recv.at[zz], above)

    def down(zz, src=None):
        s = slot(c, zz, y)
        return remote(s if src is None else src, s, down_sem.at[zz], line_recv.at[zz], below)

    def side(zz, src=None):
        s = slot(c, zz, y)
        return remote(s if src is None else src, s, y_sem.at[zz], y_recv.at[zz], beside)

    def from_side(zz):
        s = slot(c, zz, 1 - y)
        return remote(s, s, y_sem.at[zz], y_recv.at[zz], beside)

    def to_sib(zz, yy, src=None):
        s = slot(c, zz, yy)
        k = 2 * zz + yy
        return remote(s if src is None else src, s, sib_sem.at[k], sib_recv.at[k], sibling)

    def from_sib(zz, yy):
        s = slot(1 - c, zz, yy)
        k = 2 * zz + yy
        return remote(s, s, sib_sem.at[k], sib_recv.at[k], sibling)

    entry = 2 * x + c
    away = jnp.abs(z - entry)
    sends_cross = lax.div(z, 2) != x

    def cross_out():
        return remote(g_ref, cross.at[c, y], cross_sem.at[0], cross_recv.at[c],
                      (2 * (1 - x) + lax.rem(z, 2), j))

    def cross_move(k, send, recv, device):
        return remote(cross.at[k, y], cross.at[k, y], send.at[k], recv.at[k], device)

    def cross_up(k):
        return cross_move(k, cup_sem, cross_recv, above)

    def cross_down(k):
        return cross_move(k, cdown_sem, cross_recv, below)

    def cross_side(k):
        return cross_move(k, cy_sem, cy_recv, beside)

    def cross_from_side(k):
        return remote(cross.at[k, 1 - y], cross.at[k, 1 - y], cy_sem.at[k], cy_recv.at[k], beside)

    goes_up = jnp.logical_and(z >= entry, z < LINE - 1)
    goes_down = jnp.logical_and(z <= entry, z > 0)

    @pl.when(sends_cross)
    def _():
        cross_out().start()

    @pl.when(z < LINE - 1)
    def _():
        up(z, g_ref).start()

    @pl.when(z > 0)
    def _():
        down(z, g_ref).start()

    side(z, g_ref).start()
    to_sib(z, y, g_ref).start()

    piece = a_ref.shape[0] // 4

    def acts(i, index):
        start = pl.multiple_of(index * a_ref.shape[0] + i * piece, piece)
        return at_ref.at[pl.ds(start, piece)]

    def own_acts(i):
        return a_ref.at[pl.ds(i * piece, piece)]

    def acts_across(i):
        return remote(own_acts(i), acts(i, dp), ax_sem.at[i], ax_recv.at[i], across)

    def acts_from_across(i):
        s = acts(i, 2 * (1 - x) + c)
        return remote(s, s, ax_sem.at[i], ax_recv.at[i], across)

    def acts_sib(i):
        return remote(own_acts(i), acts(i, dp), as_sem.at[i], as_recv.at[i], sibling)

    def acts_from_sib(i):
        s = acts(i, 2 * x + 1 - c)
        return remote(s, s, as_sem.at[i], as_recv.at[i], sibling)

    def acts_on(i):
        s = acts(i, 2 * (1 - x) + c)
        return remote(s, s, as_sem.at[4 + i], as_recv.at[4 + i], sibling)

    def acts_on_from(i):
        s = acts(i, 2 * (1 - x) + 1 - c)
        return remote(s, s, as_sem.at[4 + i], as_recv.at[4 + i], sibling)

    def acts_local(i):
        return pltpu.make_async_copy(own_acts(i), acts(i, dp), al_sem.at[i])

    for i in range(4):
        acts_across(i).start()
    for i in range(4):
        acts_sib(i).start()
        acts_local(i).start()

    def relay_cross():
        for k in range(2):
            cross_up(k).wait_recv()

            @pl.when(goes_up)
            def _():
                cross_up(k).start()

            @pl.when(goes_down)
            def _():
                cross_down(k).start()

            cross_side(k).start()

    def pass_side(d):
        def one(zz):
            from_side(zz).wait_recv()
            to_sib(zz, 1 - y).start()

        if d == 0:
            one(z)
        else:
            pl.when(z - d >= 0)(lambda: one(z - d))
            pl.when(z + d <= LINE - 1)(lambda: one(z + d))

    for d in range(1, LINE):
        @pl.when(z - d >= 0)
        def _():
            zz = z - d
            up(zz).wait_recv()

            @pl.when(z < LINE - 1)
            def _():
                up(zz).start()

            side(zz).start()
            to_sib(zz, y).start()

        @pl.when(z + d <= LINE - 1)
        def _():
            zz = z + d
            down(zz).wait_recv()

            @pl.when(z > 0)
            def _():
                down(zz).start()

            side(zz).start()
            to_sib(zz, y).start()

        pl.when(away == d - 1)(relay_cross)
        if d >= 2:
            pass_side(d - 2)

    g_local.wait()
    for i in range(5):
        code_copy(i).wait()

    def multiply(h, first):
        for zz in range(2):
            for yy in range(2):
                from_sib(2 * h + zz, yy).wait_recv()
        base = h * half

        @pl.loop(0, half // LANES)
        def _(t):
            r = pl.ds(pl.multiple_of(base + t * LANES, LANES), LANES)
            q = pl.ds(pl.multiple_of(t * LANES, LANES), LANES)
            by = s_ref[r][None, :]
            gs[:LANES, q] = (gbuf[0, r, :].astype(F32).T * by).astype(BF16)
            gs[LANES:, q] = (gbuf[1, r, :].astype(F32).T * by).astype(BF16)

        tile = rows // 5

        @pl.loop(0, 5)
        def _(t):
            r = pl.ds(pl.multiple_of(t * tile, tile), tile)
            k = pl.ds(pl.multiple_of(base, LANES), half)
            part = lax.dot_general(
                gs[...], codes[r, k], (((1,), (1,)), ((), ())), preferred_element_type=F32)
            acc[:, r] = part if first else acc[:, r] + part

    near = lax.div(z, 2)
    multiply(near, True)
    pl.when(away == LINE - 1)(relay_cross)
    pass_side(LINE - 2)
    pass_side(LINE - 1)
    for i in range(2):
        acts_from_across(i).wait_recv()
        acts_on(i).start()
    multiply(1 - near, False)

    def tokens_of(core):
        return pl.ds(pl.multiple_of(core * LANES, LANES), LANES)

    def ig_out():
        return remote(
            acc.at[tokens_of(1 - c), pl.ds(pl.multiple_of(c * (rows - step_rows), LANES), step_rows)],
            ig_ref.at[:, pl.ds(pl.multiple_of(c * rows, LANES), step_rows)],
            ig_sem.at[0], ig_sem.at[1], sibling)

    def ig_in():
        s = ig_ref.at[:, pl.ds(pl.multiple_of((1 - c) * rows, LANES), step_rows)]
        return remote(s, s, ig_sem.at[0], ig_sem.at[1], sibling)

    ig_local = pltpu.make_async_copy(
        acc.at[tokens_of(c)], ig_ref.at[:, pl.ds(pl.multiple_of(c * step_rows, LANES), rows)], ig_sem.at[2])
    ig_out().start()
    ig_local.start()

    for i in range(2, 4):
        acts_from_across(i).wait_recv()
        acts_on(i).start()

    block = pl.ds(pl.multiple_of(2 * entry * channels, 32), 2 * channels)
    og_copies = [
        pltpu.make_async_copy(gbuf.at[k, block], og_ref.at[2 * x + k], og_sem.at[k])
        for k in range(2)
    ]
    for k in range(2):
        og_copies[k].start()
    for k in range(2):
        cross_from_side(k).wait_recv()
        for yy in range(2):
            og_copies.append(pltpu.make_async_copy(
                cross.at[k, yy], og_ref.at[2 * (1 - x) + k, pl.ds(yy * channels, channels)],
                og_sem.at[2 + 2 * k + yy]))
            og_copies[-1].start()

    for zz in range(LINE):
        @pl.when(jnp.logical_and(zz <= z, z < LINE - 1))
        def _():
            up(zz).wait_send()

        @pl.when(jnp.logical_and(zz >= z, z > 0))
        def _():
            down(zz).wait_send()

        side(zz).wait_send()
        for yy in range(2):
            to_sib(zz, yy).wait_send()

    @pl.when(sends_cross)
    def _():
        cross_out().wait_send()

    for k in range(2):
        @pl.when(goes_up)
        def _():
            cross_up(k).wait_send()

        @pl.when(goes_down)
        def _():
            cross_down(k).wait_send()

        cross_side(k).wait_send()

    for i in range(4):
        acts_across(i).wait_send()
        acts_sib(i).wait_send()
        acts_on(i).wait_send()
        acts_local(i).wait()
        acts_from_sib(i).wait_recv()
        acts_on_from(i).wait_recv()
    for copy in og_copies:
        copy.wait()
    ig_local.wait()
    ig_out().wait_send()
    ig_in().wait_recv()


TILE = 256
PARTS = 4


def weight_kernel(o_ref, a_ref, ig_ref, out_ref, ig_out, o, a, out, o_sem, a_sem, ig_sem, out_sem):
    channels = out_ref.shape[0]
    tokens = a_ref.shape[0] // 4
    loads = [pltpu.make_async_copy(o_ref.at[k], o.at[k], o_sem.at[k]) for k in range(4)]
    for k in range(4):
        rows = pl.ds(k * tokens, tokens)
        loads.append(pltpu.make_async_copy(a_ref.at[rows], a.at[rows], a_sem.at[k]))
    ig_copy = pltpu.make_async_copy(ig_ref, ig_out, ig_sem.at[0])
    for load in loads:
        load.start()
    ig_copy.start()
    for load in loads:
        load.wait()

    full = channels // TILE
    rest = channels % TILE
    n = TILE // PARTS

    def write(slot, t, i):
        start = pl.multiple_of(t * TILE + i * n, n)
        return pltpu.make_async_copy(
            out.at[slot, pl.ds(i * n, n)], out_ref.at[pl.ds(start, n)], out_sem.at[slot, i])

    def product(start, size):
        rows = pl.ds(start, size)
        left = jnp.concatenate([o[k, rows, :] for k in range(4)], axis=1)
        return jnp.dot(left, a[...], preferred_element_type=F32)

    @pl.loop(0, full)
    def _(t):
        slot = lax.rem(t, 3)

        @pl.when(t >= 3)
        def _():
            for i in range(PARTS):
                write(slot, t - 3, i).wait()

        out[slot] = product(pl.multiple_of(t * TILE, TILE), TILE)
        for i in range(PARTS):
            write(slot, t, i).start()

    last = full % 3
    for i in range(PARTS):
        write(last, full - 3, i).wait()
    out[last, :rest] = product(full * TILE, rest)
    ends = []
    for i in range(rest // n):
        ends.append(write(last, full, i))
    for end in ends:
        end.start()
    for t in (full - 2, full - 1):
        for i in range(PARTS):
            write(t % 3, t, i).wait()
    for end in ends:
        end.wait()
    ig_copy.wait()


def per_device_kernels(activations, weight_codes, channel_scale, output_grads):
    tokens, hidden = activations.shape
    channels = output_grads.shape[1]
    depth = weight_codes.shape[1]
    rows = (hidden // LANES + 1) // 2 * LANES
    dma = pltpu.SemaphoreType.DMA
    vmem = pl.BlockSpec(memory_space=pltpu.VMEM)
    anywhere = pl.BlockSpec(memory_space=pl.ANY)
    input_grads, acts, grads = pl.pallas_call(
        gather_kernel,
        out_shape=(
            jax.ShapeDtypeStruct((tokens, hidden), F32),
            jax.ShapeDtypeStruct((4 * tokens, hidden), BF16),
            jax.ShapeDtypeStruct((4, 2 * channels, tokens), BF16),
        ),
        in_specs=[anywhere, anywhere, vmem, anywhere],
        out_specs=(anywhere,) * 3,
        scratch_shapes=[
            pltpu.VMEM((rows, depth), BF16),
            pltpu.VMEM((2, depth, tokens), BF16),
            pltpu.VMEM((2, 2, channels, tokens), BF16),
            pltpu.VMEM((2 * tokens, depth // 2), BF16),
            pltpu.VMEM((2 * tokens, rows), F32),
            dma((5,)), dma((4,)), dma((4,)), dma((4,)), dma((8,)), dma((4,)), dma((4,)), dma((8,)),
            dma((1,)), dma((2,)), dma((2,)), dma((2,)), dma((2,)), dma((2,)),
            dma((4,)), dma((8,)), dma((4,)), dma((8,)), dma((4,)), dma((6,)), dma((3,)), dma((1,)),
        ],
        compiler_params=pltpu.CompilerParams(
            collective_id=0, has_side_effects=True, vmem_limit_bytes=56 * 2**20),
    )(activations, output_grads.T, channel_scale, weight_codes)
    weight_grads, input_grads = pl.pallas_call(
        weight_kernel,
        out_shape=(
            jax.ShapeDtypeStruct((2 * channels, hidden), F32),
            jax.ShapeDtypeStruct((tokens, hidden), F32),
        ),
        in_specs=[anywhere] * 3,
        out_specs=(anywhere,) * 2,
        scratch_shapes=[
            pltpu.VMEM((4, 2 * channels, tokens), BF16),
            pltpu.VMEM((4 * tokens, hidden), BF16),
            pltpu.VMEM((3, TILE, hidden), F32),
            dma((4,)), dma((4,)), dma((1,)), dma((3, PARTS)),
        ],
        compiler_params=pltpu.CompilerParams(vmem_limit_bytes=56 * 2**20),
    )(grads, acts, input_grads)
    return input_grads, weight_grads.T


def per_device_plain(activations, weight_codes, channel_scale, output_grads):
    full_rows = lax.all_gather(output_grads, "tensor", axis=1, tiled=True)
    scaled = (full_rows.astype(F32) * channel_scale).astype(BF16)
    input_grads = lax.dot_general(
        scaled, weight_codes, (((1,), (1,)), ((), ())), preferred_element_type=F32)
    grad_columns = lax.all_to_all(full_rows, "dp", split_axis=1, concat_axis=0, tiled=True)
    weight_grads = lax.dot_general(
        lax.all_gather(activations, "dp", axis=0, tiled=True), grad_columns,
        (((0,), (0,)), ((), ())), preferred_element_type=F32)
    return input_grads, weight_grads


def solution(mesh):
    placed = (P("dp", "tensor"), P("tensor", None), P(), P("dp", "tensor"))
    small = mesh.shape["dp"] == 4 and mesh.shape["tensor"] == 2 * LINE

    return jax.shard_map(
        per_device_kernels if small else per_device_plain,
        mesh=mesh,
        in_specs=placed,
        out_specs=(P("dp", "tensor"), P("tensor", "dp")),
        check_vma=False,
    )
```

```python
import functools

import jax
import jax.numpy as jnp
from jax import lax
from jax.experimental import pallas as pl
from jax.experimental.pallas import tpu as pltpu
from jax.sharding import PartitionSpec as P

MESH = pl.DeviceIdType.MESH
BF16, F32 = jnp.bfloat16, jnp.float32
LINE = 4
LANES = 128


def gather_kernel(
    a_ref, g_ref, s_ref, w_ref, ig_ref, at_ref, og_ref,
    codes, gbuf, cross, gs, scale, acc, ig_own, ig_sib, held,
    code_sem, up_sem, down_sem, y_sem, sib_sem, line_recv, y_recv, sib_recv,
    cross_sem, cup_sem, cdown_sem, cy_sem, cross_recv, cy_recv,
    ax_sem, as_sem, ax_recv, as_recv, al_sem, og_sem, ig_sem, g_sem, held_sem,
):
    dp, j = lax.axis_index("dp"), lax.axis_index("tensor")
    x, c = lax.div(dp, 2), lax.rem(dp, 2)
    z, y = lax.div(j, 2), lax.rem(j, 2)
    hidden = a_ref.shape[1]
    channels = g_ref.shape[0]
    depth = w_ref.shape[1]
    rows = codes.shape[0]
    step_rows = hidden - rows
    half = depth // 2
    sibling = (2 * x + 1 - c, j)
    across = (2 * (1 - x) + c, j)
    beside = (dp, 2 * z + 1 - y)
    above = (dp, j + 2)
    below = (dp, j - 2)

    def code_copy(i):
        n = rows // 5
        return pltpu.make_async_copy(
            w_ref.at[pl.ds(pl.multiple_of(c * step_rows + i * n, 128), n)],
            codes.at[pl.ds(i * n, n)], code_sem.at[i])

    held_load = pltpu.make_async_copy(a_ref, held.at[0], held_sem.at[0])
    held_load.start()
    barrier = pltpu.get_barrier_semaphore()

    def greet(device):
        pl.semaphore_signal(barrier, inc=1, device_id=device, device_id_type=MESH)

    greet(sibling)
    greet(beside)
    greet((2 * (1 - x), j))
    greet((2 * (1 - x) + 1, j))

    @pl.when(z < LINE - 1)
    def _():
        greet(above)

    @pl.when(z > 0)
    def _():
        greet(below)

    g_local = pltpu.make_async_copy(
        g_ref, gbuf.at[c, pl.ds(pl.multiple_of(j * channels, 32), channels)], g_sem.at[0])
    g_local.start()

    ends = jnp.logical_or(z == 0, z == LINE - 1)
    pl.semaphore_wait(barrier, jnp.where(ends, 5, 6))

    def remote(src, dst, send, recv, device):
        return pltpu.make_async_remote_copy(
            src_ref=src, dst_ref=dst, send_sem=send, recv_sem=recv,
            device_id=device, device_id_type=MESH)

    def slot(core, zz, yy):
        start = pl.multiple_of((2 * zz + yy) * channels, 32)
        return gbuf.at[core, pl.ds(start, channels)]

    def up(zz, src=None):
        s = slot(c, zz, y)
        return remote(s if src is None else src, s, up_sem.at[zz], line_recv.at[zz], above)

    def down(zz, src=None):
        s = slot(c, zz, y)
        return remote(s if src is None else src, s, down_sem.at[zz], line_recv.at[zz], below)

    def side(zz, src=None):
        s = slot(c, zz, y)
        return remote(s if src is None else src, s, y_sem.at[zz], y_recv.at[zz], beside)

    def from_side(zz):
        s = slot(c, zz, 1 - y)
        return remote(s, s, y_sem.at[zz], y_recv.at[zz], beside)

    def to_sib(zz, yy, src=None):
        s = slot(c, zz, yy)
        k = 2 * zz + yy
        return remote(s if src is None else src, s, sib_sem.at[k], sib_recv.at[k], sibling)

    def from_sib(zz, yy):
        s = slot(1 - c, zz, yy)
        k = 2 * zz + yy
        return remote(s, s, sib_sem.at[k], sib_recv.at[k], sibling)

    entry = 2 * x + c
    away = jnp.abs(z - entry)
    sends_cross = lax.div(z, 2) != x

    def cross_out():
        return remote(g_ref, cross.at[c, y], cross_sem.at[0], cross_recv.at[c],
                      (2 * (1 - x) + lax.rem(z, 2), j))

    def cross_move(k, send, recv, device):
        return remote(cross.at[k, y], cross.at[k, y], send.at[k], recv.at[k], device)

    def cross_up(k):
        return cross_move(k, cup_sem, cross_recv, above)

    def cross_down(k):
        return cross_move(k, cdown_sem, cross_recv, below)

    def cross_side(k):
        return cross_move(k, cy_sem, cy_recv, beside)

    def cross_from_side(k):
        return remote(cross.at[k, 1 - y], cross.at[k, 1 - y], cy_sem.at[k], cy_recv.at[k], beside)

    goes_up = jnp.logical_and(z >= entry, z < LINE - 1)
    goes_down = jnp.logical_and(z <= entry, z > 0)

    @pl.when(sends_cross)
    def _():
        cross_out().start()

    @pl.when(z < LINE - 1)
    def _():
        up(z, g_ref).start()

    @pl.when(z > 0)
    def _():
        down(z, g_ref).start()

    side(z, g_ref).start()
    to_sib(z, y, g_ref).start()

    piece = a_ref.shape[0] // 4

    def acts(i, index):
        start = pl.multiple_of(index * a_ref.shape[0] + i * piece, piece)
        return at_ref.at[pl.ds(start, piece)]

    def kept(k, i):
        return held.at[k, pl.ds(i * piece, piece)]

    def acts_across(i):
        return remote(kept(0, i), kept(1, i), ax_sem.at[i], ax_recv.at[i], across)

    def acts_sib(i):
        return remote(kept(0, i), acts(i, dp), as_sem.at[i], as_recv.at[i], sibling)

    def acts_from_sib(i):
        s = acts(i, 2 * x + 1 - c)
        return remote(s, s, as_sem.at[i], as_recv.at[i], sibling)

    def acts_on(i):
        return remote(
            kept(1, i), acts(i, 2 * (1 - x) + c), as_sem.at[4 + i], as_recv.at[4 + i], sibling)

    def acts_on_from(i):
        s = acts(i, 2 * (1 - x) + 1 - c)
        return remote(s, s, as_sem.at[4 + i], as_recv.at[4 + i], sibling)

    def acts_local(k, i):
        index = dp if k == 0 else 2 * (1 - x) + c
        return pltpu.make_async_copy(kept(k, i), acts(i, index), al_sem.at[4 * k + i])

    def pass_acts(i):
        acts_across(i).wait_recv()
        acts_on(i).start()
        acts_local(1, i).start()

    held_load.wait()
    for i in range(4):
        acts_across(i).start()
    for i in range(4):
        acts_sib(i).start()
        acts_local(0, i).start()

    for i in range(5):
        code_copy(i).start()

    @pl.loop(0, depth // LANES)
    def _(t):
        r = pl.ds(pl.multiple_of(t * LANES, LANES), LANES)
        scale[r, :] = jnp.broadcast_to(s_ref[r][None, :], (LANES, LANES)).T

    def relay_cross():
        for k in range(2):
            cross_up(k).wait_recv()

            @pl.when(goes_up)
            def _():
                cross_up(k).start()

            @pl.when(goes_down)
            def _():
                cross_down(k).start()

    def side_cross():
        for k in range(2):
            cross_side(k).start()

    def pass_side(d):
        def one(zz):
            from_side(zz).wait_recv()
            to_sib(zz, 1 - y).start()

        if d == 0:
            one(z)
        else:
            pl.when(z - d >= 0)(lambda: one(z - d))
            pl.when(z + d <= LINE - 1)(lambda: one(z + d))

    for d in range(1, LINE):
        @pl.when(z - d >= 0)
        def _():
            zz = z - d
            up(zz).wait_recv()

            @pl.when(z < LINE - 1)
            def _():
                up(zz).start()

            side(zz).start()
            to_sib(zz, y).start()

        @pl.when(z + d <= LINE - 1)
        def _():
            zz = z + d
            down(zz).wait_recv()

            @pl.when(z > 0)
            def _():
                down(zz).start()

            side(zz).start()
            to_sib(zz, y).start()

        pl.when(away == d - 1)(relay_cross)
        if d >= 2:
            pass_side(d - 2)

    g_local.wait()
    pl.when(away < LINE - 1)(side_cross)
    for i in range(5):
        code_copy(i).wait()

    def multiply(h, first):
        for zz in range(2):
            for yy in range(2):
                from_sib(2 * h + zz, yy).wait_recv()
        base = h * half

        @pl.loop(0, half // LANES)
        def _(t):
            r = pl.ds(pl.multiple_of(base + t * LANES, LANES), LANES)
            q = pl.ds(pl.multiple_of(t * LANES, LANES), LANES)
            by = scale[r, :]
            gs[q, :LANES] = (gbuf[0, r, :].astype(F32) * by).astype(BF16)
            gs[q, LANES:] = (gbuf[1, r, :].astype(F32) * by).astype(BF16)

        tile = rows // 5

        @pl.loop(0, 5)
        def _(t):
            r = pl.ds(pl.multiple_of(t * tile, tile), tile)
            k = pl.ds(pl.multiple_of(base, LANES), half)
            part = jnp.dot(codes[r, k], gs[...], preferred_element_type=F32)
            acc[r, :] = part if first else acc[r, :] + part

    near = lax.div(z, 2)
    multiply(near, True)

    @pl.when(away == LINE - 1)
    def _():
        relay_cross()
        side_cross()

    pass_side(LINE - 2)
    pass_side(LINE - 1)
    for i in range(2):
        pass_acts(i)
    multiply(1 - near, False)

    @pl.loop(0, rows // LANES)
    def _(t):
        r = pl.ds(pl.multiple_of(t * LANES, LANES), LANES)
        ig_sib[:, r] = acc[r, pl.ds(pl.multiple_of((1 - c) * LANES, LANES), LANES)].T
        ig_own[:, r] = acc[r, pl.ds(pl.multiple_of(c * LANES, LANES), LANES)].T

    def ig_out():
        return remote(
            ig_sib.at[:, pl.ds(pl.multiple_of(c * (rows - step_rows), LANES), step_rows)],
            ig_ref.at[:, pl.ds(pl.multiple_of(c * rows, LANES), step_rows)],
            ig_sem.at[0], ig_sem.at[1], sibling)

    def ig_in():
        s = ig_ref.at[:, pl.ds(pl.multiple_of((1 - c) * rows, LANES), step_rows)]
        return remote(s, s, ig_sem.at[0], ig_sem.at[1], sibling)

    ig_local = pltpu.make_async_copy(
        ig_own, ig_ref.at[:, pl.ds(pl.multiple_of(c * step_rows, LANES), rows)], ig_sem.at[2])
    ig_out().start()
    ig_local.start()

    for i in range(2, 4):
        pass_acts(i)

    block = pl.ds(pl.multiple_of(2 * entry * channels, 32), 2 * channels)
    og_copies = [
        pltpu.make_async_copy(gbuf.at[k, block], og_ref.at[2 * x + k], og_sem.at[k])
        for k in range(2)
    ]
    for k in range(2):
        og_copies[k].start()
    for k in range(2):
        cross_from_side(k).wait_recv()
        for yy in range(2):
            og_copies.append(pltpu.make_async_copy(
                cross.at[k, yy], og_ref.at[2 * (1 - x) + k, pl.ds(yy * channels, channels)],
                og_sem.at[2 + 2 * k + yy]))
            og_copies[-1].start()

    for zz in range(LINE):
        @pl.when(jnp.logical_and(zz <= z, z < LINE - 1))
        def _():
            up(zz).wait_send()

        @pl.when(jnp.logical_and(zz >= z, z > 0))
        def _():
            down(zz).wait_send()

        side(zz).wait_send()
        for yy in range(2):
            to_sib(zz, yy).wait_send()

    @pl.when(sends_cross)
    def _():
        cross_out().wait_send()

    for k in range(2):
        @pl.when(goes_up)
        def _():
            cross_up(k).wait_send()

        @pl.when(goes_down)
        def _():
            cross_down(k).wait_send()

        cross_side(k).wait_send()

    for i in range(4):
        acts_across(i).wait_send()
        acts_sib(i).wait_send()
        acts_on(i).wait_send()
        acts_local(0, i).wait()
        acts_local(1, i).wait()
        acts_from_sib(i).wait_recv()
        acts_on_from(i).wait_recv()
    for copy in og_copies:
        copy.wait()
    ig_local.wait()
    ig_out().wait_send()
    ig_in().wait_recv()


TILE = 256
PARTS = 4


def weight_kernel(o_ref, a_ref, ig_ref, out_ref, ig_out, o, a, out, ig, o_sem, a_sem, ig_sem, out_sem):
    channels = out_ref.shape[0]
    tokens = a_ref.shape[0] // 4
    loads = [pltpu.make_async_copy(o_ref.at[k], o.at[k], o_sem.at[k]) for k in range(4)]
    for k in range(4):
        rows = pl.ds(k * tokens, tokens)
        loads.append(pltpu.make_async_copy(a_ref.at[rows], a.at[rows], a_sem.at[k]))
    ig_in = pltpu.make_async_copy(ig_ref, ig, ig_sem.at[0])
    ig_copy = pltpu.make_async_copy(ig, ig_out, ig_sem.at[1])
    for load in loads:
        load.start()
    ig_in.start()
    for load in loads:
        load.wait()

    full = channels // TILE
    rest = channels % TILE
    n = TILE // PARTS

    def write(slot, t, i):
        start = pl.multiple_of(t * TILE + i * n, n)
        return pltpu.make_async_copy(
            out.at[slot, pl.ds(i * n, n)], out_ref.at[pl.ds(start, n)], out_sem.at[slot, i])

    def product(start, size):
        rows = pl.ds(start, size)
        left = jnp.concatenate([o[k, rows, :] for k in range(4)], axis=1)
        return jnp.dot(left, a[...], preferred_element_type=F32)

    @pl.loop(0, full)
    def _(t):
        slot = lax.rem(t, 3)

        @pl.when(t >= 3)
        def _():
            for i in range(PARTS):
                write(slot, t - 3, i).wait()

        out[slot] = product(pl.multiple_of(t * TILE, TILE), TILE)
        for i in range(PARTS):
            write(slot, t, i).start()

    ig_in.wait()
    ig_copy.start()
    last = full % 3
    for i in range(PARTS):
        write(last, full - 3, i).wait()
    out[last, :rest] = product(full * TILE, rest)
    ends = []
    for i in range(rest // n):
        ends.append(write(last, full, i))
    for end in ends:
        end.start()
    for t in (full - 2, full - 1):
        for i in range(PARTS):
            write(t % 3, t, i).wait()
    for end in ends:
        end.wait()
    ig_copy.wait()


def per_device_kernels(activations, weight_codes, channel_scale, output_grads):
    tokens, hidden = activations.shape
    channels = output_grads.shape[1]
    depth = weight_codes.shape[1]
    rows = (hidden // LANES + 1) // 2 * LANES
    dma = pltpu.SemaphoreType.DMA
    vmem = pl.BlockSpec(memory_space=pltpu.VMEM)
    anywhere = pl.BlockSpec(memory_space=pl.ANY)
    input_grads, acts, grads = pl.pallas_call(
        gather_kernel,
        out_shape=(
            jax.ShapeDtypeStruct((tokens, hidden), F32),
            jax.ShapeDtypeStruct((4 * tokens, hidden), BF16),
            jax.ShapeDtypeStruct((4, 2 * channels, tokens), BF16),
        ),
        in_specs=[anywhere, anywhere, vmem, anywhere],
        out_specs=(anywhere,) * 3,
        scratch_shapes=[
            pltpu.VMEM((rows, depth), BF16),
            pltpu.VMEM((2, depth, tokens), BF16),
            pltpu.VMEM((2, 2, channels, tokens), BF16),
            pltpu.VMEM((depth // 2, 2 * tokens), BF16),
            pltpu.VMEM((depth, LANES), F32),
            pltpu.VMEM((rows, 2 * tokens), F32),
            pltpu.VMEM((tokens, rows), F32),
            pltpu.VMEM((tokens, rows), F32),
            pltpu.VMEM((2, tokens, hidden), BF16),
            dma((5,)), dma((4,)), dma((4,)), dma((4,)), dma((8,)), dma((4,)), dma((4,)), dma((8,)),
            dma((1,)), dma((2,)), dma((2,)), dma((2,)), dma((2,)), dma((2,)),
            dma((4,)), dma((8,)), dma((4,)), dma((8,)), dma((8,)), dma((6,)), dma((3,)), dma((1,)), dma((1,)),
        ],
        compiler_params=pltpu.CompilerParams(
            collective_id=0, has_side_effects=True, vmem_limit_bytes=56 * 2**20),
    )(activations, output_grads.T, channel_scale, weight_codes)
    weight_grads, input_grads = pl.pallas_call(
        weight_kernel,
        out_shape=(
            jax.ShapeDtypeStruct((2 * channels, hidden), F32),
            jax.ShapeDtypeStruct((tokens, hidden), F32),
        ),
        in_specs=[anywhere] * 3,
        out_specs=(anywhere,) * 2,
        scratch_shapes=[
            pltpu.VMEM((4, 2 * channels, tokens), BF16),
            pltpu.VMEM((4 * tokens, hidden), BF16),
            pltpu.VMEM((3, TILE, hidden), F32),
            pltpu.VMEM((tokens, hidden), F32),
            dma((4,)), dma((4,)), dma((2,)), dma((3, PARTS)),
        ],
        compiler_params=pltpu.CompilerParams(vmem_limit_bytes=56 * 2**20),
    )(grads, acts, input_grads)
    return input_grads, weight_grads.T


def per_device_plain(activations, weight_codes, channel_scale, output_grads):
    full_rows = lax.all_gather(output_grads, "tensor", axis=1, tiled=True)
    scaled = (full_rows.astype(F32) * channel_scale).astype(BF16)
    input_grads = lax.dot_general(
        scaled, weight_codes, (((1,), (1,)), ((), ())), preferred_element_type=F32)
    grad_columns = lax.all_to_all(full_rows, "dp", split_axis=1, concat_axis=0, tiled=True)
    weight_grads = lax.dot_general(
        lax.all_gather(activations, "dp", axis=0, tiled=True), grad_columns,
        (((0,), (0,)), ((), ())), preferred_element_type=F32)
    return input_grads, weight_grads


def solution(mesh):
    placed = (P("dp", "tensor"), P("tensor", None), P(), P("dp", "tensor"))
    small = mesh.shape["dp"] == 4 and mesh.shape["tensor"] == 2 * LINE

    return jax.shard_map(
        per_device_kernels if small else per_device_plain,
        mesh=mesh,
        in_specs=placed,
        out_specs=(P("dp", "tensor"), P("tensor", "dp")),
        check_vma=False,
    )
```

```python
import functools

import jax
import jax.numpy as jnp
from jax import lax
from jax.experimental import pallas as pl
from jax.experimental.pallas import tpu as pltpu
from jax.sharding import PartitionSpec as P

MESH = pl.DeviceIdType.MESH
BF16, F32 = jnp.bfloat16, jnp.float32
LINE = 4
LANES = 128


def gather_kernel(
    a_ref, g_ref, s_ref, w_ref, ig_ref, at_ref, og_ref,
    codes, gbuf, cross, gs, scale, acc, ig_own, ig_sib, held,
    code_sem, up_sem, down_sem, y_sem, sib_sem, line_recv, y_recv, sib_recv,
    cross_sem, cup_sem, cdown_sem, cy_sem, cross_recv, cy_recv,
    ax_sem, as_sem, ax_recv, as_recv, al_sem, og_sem, ig_sem, g_sem, held_sem,
):
    dp, j = lax.axis_index("dp"), lax.axis_index("tensor")
    x, c = lax.div(dp, 2), lax.rem(dp, 2)
    z, y = lax.div(j, 2), lax.rem(j, 2)
    hidden = a_ref.shape[1]
    channels = g_ref.shape[0]
    depth = w_ref.shape[1]
    rows = codes.shape[0]
    step_rows = hidden - rows
    sibling = (2 * x + 1 - c, j)
    across = (2 * (1 - x) + c, j)
    beside = (dp, 2 * z + 1 - y)
    above = (dp, j + 2)
    below = (dp, j - 2)

    def code_copy(i):
        n = rows // 5
        return pltpu.make_async_copy(
            w_ref.at[pl.ds(pl.multiple_of(c * step_rows + i * n, 128), n)],
            codes.at[pl.ds(i * n, n)], code_sem.at[i])

    held_load = pltpu.make_async_copy(a_ref, held.at[0], held_sem.at[0])
    held_load.start()
    barrier = pltpu.get_barrier_semaphore()

    def greet(device):
        pl.semaphore_signal(barrier, inc=1, device_id=device, device_id_type=MESH)

    greet(sibling)
    greet(beside)
    greet((2 * (1 - x), j))
    greet((2 * (1 - x) + 1, j))

    @pl.when(z < LINE - 1)
    def _():
        greet(above)

    @pl.when(z > 0)
    def _():
        greet(below)

    g_local = pltpu.make_async_copy(
        g_ref, gbuf.at[c, pl.ds(pl.multiple_of(j * channels, 32), channels)], g_sem.at[0])
    g_local.start()

    ends = jnp.logical_or(z == 0, z == LINE - 1)
    pl.semaphore_wait(barrier, jnp.where(ends, 5, 6))

    def remote(src, dst, send, recv, device):
        return pltpu.make_async_remote_copy(
            src_ref=src, dst_ref=dst, send_sem=send, recv_sem=recv,
            device_id=device, device_id_type=MESH)

    def slot(core, zz, yy):
        start = pl.multiple_of((2 * zz + yy) * channels, 32)
        return gbuf.at[core, pl.ds(start, channels)]

    def up(zz, src=None):
        s = slot(c, zz, y)
        return remote(s if src is None else src, s, up_sem.at[zz], line_recv.at[zz], above)

    def down(zz, src=None):
        s = slot(c, zz, y)
        return remote(s if src is None else src, s, down_sem.at[zz], line_recv.at[zz], below)

    def side(zz, src=None):
        s = slot(c, zz, y)
        return remote(s if src is None else src, s, y_sem.at[zz], y_recv.at[zz], beside)

    def from_side(zz):
        s = slot(c, zz, 1 - y)
        return remote(s, s, y_sem.at[zz], y_recv.at[zz], beside)

    def to_sib(zz, yy, src=None):
        s = slot(c, zz, yy)
        k = 2 * zz + yy
        return remote(s if src is None else src, s, sib_sem.at[k], sib_recv.at[k], sibling)

    def from_sib(zz, yy):
        s = slot(1 - c, zz, yy)
        k = 2 * zz + yy
        return remote(s, s, sib_sem.at[k], sib_recv.at[k], sibling)

    entry = 2 * x + c
    away = jnp.abs(z - entry)
    sends_cross = lax.div(z, 2) != x

    def cross_out():
        return remote(g_ref, cross.at[c, y], cross_sem.at[0], cross_recv.at[c],
                      (2 * (1 - x) + lax.rem(z, 2), j))

    def cross_move(k, send, recv, device):
        return remote(cross.at[k, y], cross.at[k, y], send.at[k], recv.at[k], device)

    def cross_up(k):
        return cross_move(k, cup_sem, cross_recv, above)

    def cross_down(k):
        return cross_move(k, cdown_sem, cross_recv, below)

    def cross_side(k):
        return cross_move(k, cy_sem, cy_recv, beside)

    def cross_from_side(k):
        return remote(cross.at[k, 1 - y], cross.at[k, 1 - y], cy_sem.at[k], cy_recv.at[k], beside)

    goes_up = jnp.logical_and(z >= entry, z < LINE - 1)
    goes_down = jnp.logical_and(z <= entry, z > 0)

    @pl.when(sends_cross)
    def _():
        cross_out().start()

    @pl.when(z < LINE - 1)
    def _():
        up(z, g_ref).start()

    @pl.when(z > 0)
    def _():
        down(z, g_ref).start()

    side(z, g_ref).start()
    to_sib(z, y, g_ref).start()

    piece = a_ref.shape[0] // 4

    def acts(i, index):
        start = pl.multiple_of(index * a_ref.shape[0] + i * piece, piece)
        return at_ref.at[pl.ds(start, piece)]

    def kept(k, i):
        return held.at[k, pl.ds(i * piece, piece)]

    def acts_across(i):
        return remote(kept(0, i), kept(1, i), ax_sem.at[i], ax_recv.at[i], across)

    def acts_sib(i):
        return remote(kept(0, i), acts(i, dp), as_sem.at[i], as_recv.at[i], sibling)

    def acts_from_sib(i):
        s = acts(i, 2 * x + 1 - c)
        return remote(s, s, as_sem.at[i], as_recv.at[i], sibling)

    def acts_on(i):
        return remote(
            kept(1, i), acts(i, 2 * (1 - x) + c), as_sem.at[4 + i], as_recv.at[4 + i], sibling)

    def acts_on_from(i):
        s = acts(i, 2 * (1 - x) + 1 - c)
        return remote(s, s, as_sem.at[4 + i], as_recv.at[4 + i], sibling)

    def acts_local(k, i):
        index = dp if k == 0 else 2 * (1 - x) + c
        return pltpu.make_async_copy(kept(k, i), acts(i, index), al_sem.at[4 * k + i])

    def pass_acts(i):
        acts_across(i).wait_recv()
        acts_on(i).start()
        acts_local(1, i).start()

    held_load.wait()
    for i in range(4):
        acts_across(i).start()
    for i in range(4):
        acts_sib(i).start()
        acts_local(0, i).start()

    for i in range(5):
        code_copy(i).start()

    @pl.loop(0, depth // LANES)
    def _(t):
        r = pl.ds(pl.multiple_of(t * LANES, LANES), LANES)
        scale[r, :] = jnp.broadcast_to(s_ref[r][None, :], (LANES, LANES)).T

    def relay_cross():
        for k in range(2):
            cross_up(k).wait_recv()

            @pl.when(goes_up)
            def _():
                cross_up(k).start()

            @pl.when(goes_down)
            def _():
                cross_down(k).start()

    def side_cross():
        for k in range(2):
            cross_side(k).start()

    pair = 2 * channels
    span = gs.shape[1]
    tile = rows // 5

    def multiply(zz, first, final):
        for yy in range(2):
            from_sib(zz, yy).wait_recv()
        begin = pl.multiple_of(zz * pair, 64)
        shift = pl.multiple_of((span - pair) * lax.rem(zz, 2), 64)
        gs[zz, pl.ds(pl.multiple_of((1 - lax.rem(zz, 2)) * pair, 64), span - pair), :] = (
            jnp.zeros((span - pair, 2 * LANES), BF16))

        @pl.loop(0, pair // 64)
        def _(t):
            r = pl.ds(pl.multiple_of(begin + t * 64, 64), 64)
            q = pl.ds(pl.multiple_of(shift + t * 64, 64), 64)
            by = scale[r, :]
            gs[zz, q, :LANES] = (gbuf[0, r, :].astype(F32) * by).astype(BF16)
            gs[zz, q, LANES:] = (gbuf[1, r, :].astype(F32) * by).astype(BF16)

        k = pl.ds(pl.multiple_of(lax.div(zz * pair, LANES) * LANES, LANES), span)

        @pl.loop(0, 5)
        def _(t):
            if first:
                code_copy(t).wait()
            r = pl.ds(pl.multiple_of(t * tile, tile), tile)
            part = jnp.dot(codes[r, k], gs[zz], preferred_element_type=F32)
            if not first:
                part = acc[r, :] + part
            acc[r, :] = part
            if final:
                ig_sib[:, r] = acc[r, pl.ds(pl.multiple_of((1 - c) * LANES, LANES), LANES)].T
                ig_own[:, r] = acc[r, pl.ds(pl.multiple_of(c * LANES, LANES), LANES)].T

    def pass_side(zz):
        from_side(zz).wait_recv()
        to_sib(zz, 1 - y).start()

    def relay(d):
        @pl.when(z - d >= 0)
        def _():
            zz = z - d
            up(zz).wait_recv()

            @pl.when(z < LINE - 1)
            def _():
                up(zz).start()

            side(zz).start()
            to_sib(zz, y).start()

        @pl.when(z + d <= LINE - 1)
        def _():
            zz = z + d
            down(zz).wait_recv()

            @pl.when(z > 0)
            def _():
                down(zz).start()

            side(zz).start()
            to_sib(zz, y).start()

        pl.when(away == d - 1)(relay_cross)

    low = z < LINE // 2
    end = jnp.logical_or(z == 0, z == LINE - 1)
    second = jnp.where(z > 0, z - 1, 1)
    third = jnp.where(end, jnp.where(low, 2, 1), z + 1)
    fourth = jnp.where(low, LINE - 1, 0)

    relay(1)
    g_local.wait()
    pass_side(z)
    multiply(z, True, False)
    relay(2)
    pass_side(second)
    multiply(second, False, False)
    relay(3)
    pl.when(away < LINE - 1)(side_cross)
    pass_side(third)
    multiply(third, False, False)

    @pl.when(away == LINE - 1)
    def _():
        relay_cross()
        side_cross()

    for i in range(2):
        pass_acts(i)
    pass_side(fourth)
    multiply(fourth, False, True)

    def ig_out():
        return remote(
            ig_sib.at[:, pl.ds(pl.multiple_of(c * (rows - step_rows), LANES), step_rows)],
            ig_ref.at[:, pl.ds(pl.multiple_of(c * rows, LANES), step_rows)],
            ig_sem.at[0], ig_sem.at[1], sibling)

    def ig_in():
        s = ig_ref.at[:, pl.ds(pl.multiple_of((1 - c) * rows, LANES), step_rows)]
        return remote(s, s, ig_sem.at[0], ig_sem.at[1], sibling)

    ig_local = pltpu.make_async_copy(
        ig_own, ig_ref.at[:, pl.ds(pl.multiple_of(c * step_rows, LANES), rows)], ig_sem.at[2])
    ig_out().start()
    ig_local.start()

    for i in range(2, 4):
        pass_acts(i)

    block = pl.ds(pl.multiple_of(2 * entry * channels, 32), 2 * channels)
    og_copies = [
        pltpu.make_async_copy(gbuf.at[k, block], og_ref.at[2 * x + k], og_sem.at[k])
        for k in range(2)
    ]
    for k in range(2):
        og_copies[k].start()
    for k in range(2):
        cross_from_side(k).wait_recv()
        for yy in range(2):
            og_copies.append(pltpu.make_async_copy(
                cross.at[k, yy], og_ref.at[2 * (1 - x) + k, pl.ds(yy * channels, channels)],
                og_sem.at[2 + 2 * k + yy]))
            og_copies[-1].start()

    for zz in range(LINE):
        @pl.when(jnp.logical_and(zz <= z, z < LINE - 1))
        def _():
            up(zz).wait_send()

        @pl.when(jnp.logical_and(zz >= z, z > 0))
        def _():
            down(zz).wait_send()

        side(zz).wait_send()
        for yy in range(2):
            to_sib(zz, yy).wait_send()

    @pl.when(sends_cross)
    def _():
        cross_out().wait_send()

    for k in range(2):
        @pl.when(goes_up)
        def _():
            cross_up(k).wait_send()

        @pl.when(goes_down)
        def _():
            cross_down(k).wait_send()

        cross_side(k).wait_send()

    for i in range(4):
        acts_across(i).wait_send()
        acts_sib(i).wait_send()
        acts_on(i).wait_send()
        acts_local(0, i).wait()
        acts_local(1, i).wait()
        acts_from_sib(i).wait_recv()
        acts_on_from(i).wait_recv()
    for copy in og_copies:
        copy.wait()
    ig_local.wait()
    ig_out().wait_send()
    ig_in().wait_recv()


WIDE = 512
PARTS = 4


def weight_kernel(o_ref, a_ref, ig_ref, out_ref, ig_out, o, a, out, ig, o_sem, a_sem, ig_sem, out_sem):
    channels, hidden = out_ref.shape
    full, rest = hidden // WIDE, hidden % WIDE
    n = channels // PARTS

    def load_a(t, width):
        columns = pl.ds(pl.multiple_of(t * WIDE, LANES), width)
        return pltpu.make_async_copy(a_ref.at[:, columns], a.at[:, columns], a_sem.at[t])

    loads = [pltpu.make_async_copy(o_ref.at[k], o.at[k], o_sem.at[k]) for k in range(4)]
    ig_in = pltpu.make_async_copy(ig_ref, ig, ig_sem.at[0])
    ig_copy = pltpu.make_async_copy(ig, ig_out, ig_sem.at[1])
    load_a(0, WIDE).start()
    for load in loads:
        load.start()
    for t in range(1, full):
        load_a(t, WIDE).start()
    load_a(full, rest).start()
    ig_in.start()
    for load in loads:
        load.wait()

    def write(slot, t, i, width=WIDE):
        rows = pl.ds(pl.multiple_of(i * n, 16), n)
        return pltpu.make_async_copy(
            out.at[slot, rows, pl.ds(0, width)],
            out_ref.at[rows, pl.ds(pl.multiple_of(t * WIDE, LANES), width)], out_sem.at[slot, i])

    def work(slot, t, width):
        columns = pl.ds(pl.multiple_of(t * WIDE, LANES), width)

        @pl.loop(0, PARTS)
        def _(i):
            rows = pl.ds(pl.multiple_of(i * n, 16), n)
            left = jnp.concatenate([o[k, rows, :] for k in range(4)], axis=1)
            out[slot, rows, :width] = jnp.dot(left, a[:, columns], preferred_element_type=F32)
            write(slot, t, i, width).start()

    @pl.loop(0, full)
    def _(t):
        slot = lax.rem(t, 3)

        @pl.when(t >= 3)
        def _():
            for i in range(PARTS):
                write(slot, t - 3, i).wait()

        load_a(t, WIDE).wait()
        work(slot, t, WIDE)

    ig_in.wait()
    ig_copy.start()
    last = full % 3
    for i in range(PARTS):
        write(last, full - 3, i).wait()
    load_a(full, rest).wait()
    work(last, full, rest)
    for t in (full - 2, full - 1):
        for i in range(PARTS):
            write(t % 3, t, i).wait()
    for i in range(PARTS):
        write(last, full, i, rest).wait()
    ig_copy.wait()


def per_device_kernels(activations, weight_codes, channel_scale, output_grads):
    tokens, hidden = activations.shape
    channels = output_grads.shape[1]
    depth = weight_codes.shape[1]
    rows = (hidden // LANES + 1) // 2 * LANES
    dma = pltpu.SemaphoreType.DMA
    vmem = pl.BlockSpec(memory_space=pltpu.VMEM)
    anywhere = pl.BlockSpec(memory_space=pl.ANY)
    input_grads, acts, grads = pl.pallas_call(
        gather_kernel,
        out_shape=(
            jax.ShapeDtypeStruct((tokens, hidden), F32),
            jax.ShapeDtypeStruct((4 * tokens, hidden), BF16),
            jax.ShapeDtypeStruct((4, 2 * channels, tokens), BF16),
        ),
        in_specs=[anywhere, anywhere, vmem, anywhere],
        out_specs=(anywhere,) * 3,
        scratch_shapes=[
            pltpu.VMEM((rows, depth), BF16),
            pltpu.VMEM((2, depth, tokens), BF16),
            pltpu.VMEM((2, 2, channels, tokens), BF16),
            pltpu.VMEM((LINE, pl.cdiv(2 * channels, LANES) * LANES, 2 * tokens), BF16),
            pltpu.VMEM((depth, LANES), F32),
            pltpu.VMEM((rows, 2 * tokens), F32),
            pltpu.VMEM((tokens, rows), F32),
            pltpu.VMEM((tokens, rows), F32),
            pltpu.VMEM((2, tokens, hidden), BF16),
            dma((5,)), dma((4,)), dma((4,)), dma((4,)), dma((8,)), dma((4,)), dma((4,)), dma((8,)),
            dma((1,)), dma((2,)), dma((2,)), dma((2,)), dma((2,)), dma((2,)),
            dma((4,)), dma((8,)), dma((4,)), dma((8,)), dma((8,)), dma((6,)), dma((3,)), dma((1,)), dma((1,)),
        ],
        compiler_params=pltpu.CompilerParams(
            collective_id=0, has_side_effects=True, vmem_limit_bytes=56 * 2**20),
    )(activations, output_grads.T, channel_scale, weight_codes)
    weight_grads, input_grads = pl.pallas_call(
        weight_kernel,
        out_shape=(
            jax.ShapeDtypeStruct((2 * channels, hidden), F32),
            jax.ShapeDtypeStruct((tokens, hidden), F32),
        ),
        in_specs=[anywhere] * 3,
        out_specs=(anywhere,) * 2,
        scratch_shapes=[
            pltpu.VMEM((4, 2 * channels, tokens), BF16),
            pltpu.VMEM((4 * tokens, hidden), BF16),
            pltpu.VMEM((3, 2 * channels, WIDE), F32),
            pltpu.VMEM((tokens, hidden), F32),
            dma((4,)), dma((hidden // WIDE + 1,)), dma((2,)), dma((3, PARTS)),
        ],
        compiler_params=pltpu.CompilerParams(vmem_limit_bytes=56 * 2**20),
    )(grads, acts, input_grads)
    return input_grads, weight_grads.T


def per_device_plain(activations, weight_codes, channel_scale, output_grads):
    full_rows = lax.all_gather(output_grads, "tensor", axis=1, tiled=True)
    scaled = (full_rows.astype(F32) * channel_scale).astype(BF16)
    input_grads = lax.dot_general(
        scaled, weight_codes, (((1,), (1,)), ((), ())), preferred_element_type=F32)
    grad_columns = lax.all_to_all(full_rows, "dp", split_axis=1, concat_axis=0, tiled=True)
    weight_grads = lax.dot_general(
        lax.all_gather(activations, "dp", axis=0, tiled=True), grad_columns,
        (((0,), (0,)), ((), ())), preferred_element_type=F32)
    return input_grads, weight_grads


def solution(mesh):
    placed = (P("dp", "tensor"), P("tensor", None), P(), P("dp", "tensor"))
    small = mesh.shape["dp"] == 4 and mesh.shape["tensor"] == 2 * LINE

    return jax.shard_map(
        per_device_kernels if small else per_device_plain,
        mesh=mesh,
        in_specs=placed,
        out_specs=(P("dp", "tensor"), P("tensor", "dp")),
        check_vma=False,
    )
```

```python
import functools

import jax
import jax.numpy as jnp
from jax import lax
from jax.experimental import pallas as pl
from jax.experimental.pallas import tpu as pltpu
from jax.sharding import PartitionSpec as P

MESH = pl.DeviceIdType.MESH
BF16, F32 = jnp.bfloat16, jnp.float32
LINE = 4
LANES = 128


def gather_kernel(
    a_ref, g_ref, s_ref, w_ref, ig_ref, at_ref, og_ref,
    codes, gbuf, cross, gs, scale, acc, ig_own, ig_sib, held,
    code_sem, up_sem, down_sem, y_sem, sib_sem, line_recv, y_recv, sib_recv,
    cross_sem, cup_sem, cdown_sem, cy_sem, cross_recv, cy_recv,
    ax_sem, as_sem, ax_recv, as_recv, al_sem, og_sem, ig_sem, g_sem, held_sem, far_sem,
):
    dp, j = lax.axis_index("dp"), lax.axis_index("tensor")
    x, c = lax.div(dp, 2), lax.rem(dp, 2)
    z, y = lax.div(j, 2), lax.rem(j, 2)
    hidden = a_ref.shape[1]
    channels = g_ref.shape[0]
    depth = w_ref.shape[1]
    rows = codes.shape[0]
    step_rows = hidden - rows
    sibling = (2 * x + 1 - c, j)
    across = (2 * (1 - x) + c, j)
    beside = (dp, 2 * z + 1 - y)
    above = (dp, j + 2)
    below = (dp, j - 2)

    def code_copy(i):
        n = rows // 5
        return pltpu.make_async_copy(
            w_ref.at[pl.ds(pl.multiple_of(c * step_rows + i * n, 128), n)],
            codes.at[pl.ds(i * n, n)], code_sem.at[i])

    held_load = pltpu.make_async_copy(a_ref, held.at[0], held_sem.at[0])
    held_load.start()
    barrier = pltpu.get_barrier_semaphore()

    def greet(device):
        pl.semaphore_signal(barrier, inc=1, device_id=device, device_id_type=MESH)

    greet(sibling)
    greet(beside)
    greet((2 * (1 - x), j))
    greet((2 * (1 - x) + 1, j))

    @pl.when(z < LINE - 1)
    def _():
        greet(above)

    @pl.when(z > 0)
    def _():
        greet(below)

    g_local = pltpu.make_async_copy(
        g_ref, gbuf.at[c, pl.ds(pl.multiple_of(j * channels, 32), channels)], g_sem.at[0])
    g_local.start()

    ends = jnp.logical_or(z == 0, z == LINE - 1)
    pl.semaphore_wait(barrier, jnp.where(ends, 5, 6))

    def remote(src, dst, send, recv, device):
        return pltpu.make_async_remote_copy(
            src_ref=src, dst_ref=dst, send_sem=send, recv_sem=recv,
            device_id=device, device_id_type=MESH)

    def slot(core, zz, yy):
        start = pl.multiple_of((2 * zz + yy) * channels, 32)
        return gbuf.at[core, pl.ds(start, channels)]

    def up(zz, src=None):
        s = slot(c, zz, y)
        return remote(s if src is None else src, s, up_sem.at[zz], line_recv.at[zz], above)

    def down(zz, src=None):
        s = slot(c, zz, y)
        return remote(s if src is None else src, s, down_sem.at[zz], line_recv.at[zz], below)

    def side(zz, src=None):
        s = slot(c, zz, y)
        return remote(s if src is None else src, s, y_sem.at[zz], y_recv.at[zz], beside)

    def from_side(zz):
        s = slot(c, zz, 1 - y)
        return remote(s, s, y_sem.at[zz], y_recv.at[zz], beside)

    def to_sib(zz, yy, src=None):
        s = slot(c, zz, yy)
        k = 2 * zz + yy
        return remote(s if src is None else src, s, sib_sem.at[k], sib_recv.at[k], sibling)

    def from_sib(zz, yy):
        s = slot(1 - c, zz, yy)
        k = 2 * zz + yy
        return remote(s, s, sib_sem.at[k], sib_recv.at[k], sibling)

    entry = 2 * x + c
    away = jnp.abs(z - entry)
    sends_cross = lax.div(z, 2) != x

    def cross_out():
        return remote(g_ref, cross.at[c, y], cross_sem.at[0], cross_recv.at[c],
                      (2 * (1 - x) + lax.rem(z, 2), j))

    def cross_move(k, send, recv, device):
        return remote(cross.at[k, y], cross.at[k, y], send.at[k], recv.at[k], device)

    def cross_up(k):
        return cross_move(k, cup_sem, cross_recv, above)

    def cross_down(k):
        return cross_move(k, cdown_sem, cross_recv, below)

    def cross_side(k):
        return cross_move(k, cy_sem, cy_recv, beside)

    def cross_from_side(k):
        return remote(cross.at[k, 1 - y], cross.at[k, 1 - y], cy_sem.at[k], cy_recv.at[k], beside)

    goes_up = jnp.logical_and(z >= entry, z < LINE - 1)
    goes_down = jnp.logical_and(z <= entry, z > 0)

    @pl.when(sends_cross)
    def _():
        cross_out().start()

    @pl.when(z < LINE - 1)
    def _():
        up(z, g_ref).start()

    @pl.when(z > 0)
    def _():
        down(z, g_ref).start()

    side(z, g_ref).start()
    to_sib(z, y, g_ref).start()

    piece = a_ref.shape[0] // 4

    def acts(i, index):
        start = pl.multiple_of(index * a_ref.shape[0] + i * piece, piece)
        return at_ref.at[pl.ds(start, piece)]

    def kept(k, i):
        return held.at[k, pl.ds(i * piece, piece)]

    def acts_across(i):
        return remote(kept(0, i), kept(1, i), ax_sem.at[i], ax_recv.at[i], across)

    def acts_sib(i):
        return remote(kept(0, i), acts(i, dp), as_sem.at[i], as_recv.at[i], sibling)

    def acts_from_sib(i):
        s = acts(i, 2 * x + 1 - c)
        return remote(s, s, as_sem.at[i], as_recv.at[i], sibling)

    def acts_on(i):
        return remote(
            kept(1, i), acts(i, 2 * (1 - x) + c), as_sem.at[4 + i], as_recv.at[4 + i], sibling)

    def acts_on_from(i):
        s = acts(i, 2 * (1 - x) + 1 - c)
        return remote(s, s, as_sem.at[4 + i], as_recv.at[4 + i], sibling)

    def acts_local(k, i):
        index = dp if k == 0 else 2 * (1 - x) + c
        return pltpu.make_async_copy(kept(k, i), acts(i, index), al_sem.at[4 * k + i])

    def pass_acts(i):
        acts_across(i).wait_recv()
        acts_on(i).start()
        acts_local(1, i).start()

    held_load.wait()
    for i in range(4):
        acts_across(i).start()
    for i in range(4):
        acts_sib(i).start()
        acts_local(0, i).start()

    for i in range(5):
        code_copy(i).start()

    @pl.loop(0, depth // LANES)
    def _(t):
        r = pl.ds(pl.multiple_of(t * LANES, LANES), LANES)
        scale[r, :] = jnp.broadcast_to(s_ref[r][None, :], (LANES, LANES)).T

    def relay_cross():
        for k in range(2):
            cross_up(k).wait_recv()

            @pl.when(goes_up)
            def _():
                cross_up(k).start()

            @pl.when(goes_down)
            def _():
                cross_down(k).start()

    def side_cross():
        for k in range(2):
            cross_side(k).start()

    pair = 2 * channels
    span = gs.shape[1]
    tile = rows // 5

    def multiply(zz, first, final):
        for yy in range(2):
            from_sib(zz, yy).wait_recv()
        begin = pl.multiple_of(zz * pair, 64)
        shift = pl.multiple_of((span - pair) * lax.rem(zz, 2), 64)
        gs[zz, pl.ds(pl.multiple_of((1 - lax.rem(zz, 2)) * pair, 64), span - pair), :] = (
            jnp.zeros((span - pair, 2 * LANES), BF16))

        @pl.loop(0, pair // 64)
        def _(t):
            r = pl.ds(pl.multiple_of(begin + t * 64, 64), 64)
            q = pl.ds(pl.multiple_of(shift + t * 64, 64), 64)
            by = scale[r, :]
            gs[zz, q, :LANES] = (gbuf[0, r, :].astype(F32) * by).astype(BF16)
            gs[zz, q, LANES:] = (gbuf[1, r, :].astype(F32) * by).astype(BF16)

        k = pl.ds(pl.multiple_of(lax.div(zz * pair, LANES) * LANES, LANES), span)

        @pl.loop(0, 5)
        def _(t):
            if first:
                code_copy(t).wait()
            r = pl.ds(pl.multiple_of(t * tile, tile), tile)
            part = jnp.dot(codes[r, k], gs[zz], preferred_element_type=F32)
            if not first:
                part = acc[r, :] + part
            acc[r, :] = part
            if final:
                ig_sib[:, r] = acc[r, pl.ds(pl.multiple_of((1 - c) * LANES, LANES), LANES)].T
                ig_own[:, r] = acc[r, pl.ds(pl.multiple_of(c * LANES, LANES), LANES)].T

    def pass_side(zz):
        from_side(zz).wait_recv()
        to_sib(zz, 1 - y).start()

    def relay(d):
        @pl.when(z - d >= 0)
        def _():
            zz = z - d
            up(zz).wait_recv()

            @pl.when(z < LINE - 1)
            def _():
                up(zz).start()

            side(zz).start()
            to_sib(zz, y).start()

        @pl.when(z + d <= LINE - 1)
        def _():
            zz = z + d
            down(zz).wait_recv()

            @pl.when(z > 0)
            def _():
                down(zz).start()

            side(zz).start()
            to_sib(zz, y).start()

        pl.when(away == d - 1)(relay_cross)

    low = z < LINE // 2
    end = jnp.logical_or(z == 0, z == LINE - 1)
    second = jnp.where(z > 0, z - 1, 1)
    third = jnp.where(end, jnp.where(low, 2, 1), z + 1)
    fourth = jnp.where(low, LINE - 1, 0)

    relay(1)
    g_local.wait()
    pass_side(z)
    multiply(z, True, False)
    relay(2)
    pass_side(second)
    multiply(second, False, False)
    relay(3)
    pl.when(away < LINE - 1)(side_cross)
    pass_side(third)
    multiply(third, False, False)

    for i in range(2):
        pass_acts(i)
    pass_side(fourth)

    sends_far = jnp.logical_and(end, jnp.logical_not(sends_cross))

    def far_out():
        return remote(slot(c, fourth, 1 - y), cross.at[c, 1 - y], far_sem.at[0], cy_recv.at[c],
                      (2 * (1 - x) + lax.rem(fourth, 2), j))

    @pl.when(sends_far)
    def _():
        far_out().start()

    multiply(fourth, False, True)

    def ig_out():
        return remote(
            ig_sib.at[:, pl.ds(pl.multiple_of(c * (rows - step_rows), LANES), step_rows)],
            ig_ref.at[:, pl.ds(pl.multiple_of(c * rows, LANES), step_rows)],
            ig_sem.at[0], ig_sem.at[1], sibling)

    def ig_in():
        s = ig_ref.at[:, pl.ds(pl.multiple_of((1 - c) * rows, LANES), step_rows)]
        return remote(s, s, ig_sem.at[0], ig_sem.at[1], sibling)

    ig_local = pltpu.make_async_copy(
        ig_own, ig_ref.at[:, pl.ds(pl.multiple_of(c * step_rows, LANES), rows)], ig_sem.at[2])
    ig_out().start()
    ig_local.start()

    for i in range(2, 4):
        pass_acts(i)

    pl.when(away == LINE - 1)(relay_cross)

    block = pl.ds(pl.multiple_of(2 * entry * channels, 32), 2 * channels)
    og_copies = [
        pltpu.make_async_copy(gbuf.at[k, block], og_ref.at[2 * x + k], og_sem.at[k])
        for k in range(2)
    ]
    for k in range(2):
        og_copies[k].start()
    for k in range(2):
        cross_from_side(k).wait_recv()
        for yy in range(2):
            og_copies.append(pltpu.make_async_copy(
                cross.at[k, yy], og_ref.at[2 * (1 - x) + k, pl.ds(yy * channels, channels)],
                og_sem.at[2 + 2 * k + yy]))
            og_copies[-1].start()

    for zz in range(LINE):
        @pl.when(jnp.logical_and(zz <= z, z < LINE - 1))
        def _():
            up(zz).wait_send()

        @pl.when(jnp.logical_and(zz >= z, z > 0))
        def _():
            down(zz).wait_send()

        side(zz).wait_send()
        for yy in range(2):
            to_sib(zz, yy).wait_send()

    @pl.when(sends_cross)
    def _():
        cross_out().wait_send()

    for k in range(2):
        @pl.when(goes_up)
        def _():
            cross_up(k).wait_send()

        @pl.when(goes_down)
        def _():
            cross_down(k).wait_send()

        @pl.when(away < LINE - 1)
        def _():
            cross_side(k).wait_send()

    @pl.when(sends_far)
    def _():
        far_out().wait_send()

    for i in range(4):
        acts_across(i).wait_send()
        acts_sib(i).wait_send()
        acts_on(i).wait_send()
        acts_local(0, i).wait()
        acts_local(1, i).wait()
        acts_from_sib(i).wait_recv()
        acts_on_from(i).wait_recv()
    for copy in og_copies:
        copy.wait()
    ig_local.wait()
    ig_out().wait_send()
    ig_in().wait_recv()


TILE = 256
PARTS = 4


def weight_kernel(o_ref, a_ref, ig_ref, out_ref, ig_out, o, a, out, ig, o_sem, a_sem, ig_sem, out_sem):
    channels = out_ref.shape[0]
    tokens = a_ref.shape[0] // 4
    loads = [pltpu.make_async_copy(o_ref.at[k], o.at[k], o_sem.at[k]) for k in range(4)]
    for k in range(4):
        rows = pl.ds(k * tokens, tokens)
        loads.append(pltpu.make_async_copy(a_ref.at[rows], a.at[rows], a_sem.at[k]))
    ig_in = pltpu.make_async_copy(ig_ref, ig, ig_sem.at[0])
    ig_copy = pltpu.make_async_copy(ig, ig_out, ig_sem.at[1])
    for load in loads:
        load.start()
    ig_in.start()
    for load in loads:
        load.wait()

    full = channels // TILE
    rest = channels % TILE
    n = TILE // PARTS

    def write(slot, t, i):
        start = pl.multiple_of(t * TILE + i * n, n)
        return pltpu.make_async_copy(
            out.at[slot, pl.ds(i * n, n)], out_ref.at[pl.ds(start, n)], out_sem.at[slot, i])

    def product(start, size):
        rows = pl.ds(start, size)
        left = jnp.concatenate([o[k, rows, :] for k in range(4)], axis=1)
        return jnp.dot(left, a[...], preferred_element_type=F32)

    @pl.loop(0, full)
    def _(t):
        slot = lax.rem(t, 3)

        @pl.when(t >= 3)
        def _():
            for i in range(PARTS):
                write(slot, t - 3, i).wait()

        out[slot] = product(pl.multiple_of(t * TILE, TILE), TILE)
        for i in range(PARTS):
            write(slot, t, i).start()

    ig_in.wait()
    ig_copy.start()
    last = full % 3
    for i in range(PARTS):
        write(last, full - 3, i).wait()
    out[last, :rest] = product(full * TILE, rest)
    ends = []
    for i in range(rest // n):
        ends.append(write(last, full, i))
    for end in ends:
        end.start()
    for t in (full - 2, full - 1):
        for i in range(PARTS):
            write(t % 3, t, i).wait()
    for end in ends:
        end.wait()
    ig_copy.wait()


def per_device_kernels(activations, weight_codes, channel_scale, output_grads):
    tokens, hidden = activations.shape
    channels = output_grads.shape[1]
    depth = weight_codes.shape[1]
    rows = (hidden // LANES + 1) // 2 * LANES
    dma = pltpu.SemaphoreType.DMA
    vmem = pl.BlockSpec(memory_space=pltpu.VMEM)
    anywhere = pl.BlockSpec(memory_space=pl.ANY)
    input_grads, acts, grads = pl.pallas_call(
        gather_kernel,
        out_shape=(
            jax.ShapeDtypeStruct((tokens, hidden), F32),
            jax.ShapeDtypeStruct((4 * tokens, hidden), BF16),
            jax.ShapeDtypeStruct((4, 2 * channels, tokens), BF16),
        ),
        in_specs=[anywhere, anywhere, vmem, anywhere],
        out_specs=(anywhere,) * 3,
        scratch_shapes=[
            pltpu.VMEM((rows, depth), BF16),
            pltpu.VMEM((2, depth, tokens), BF16),
            pltpu.VMEM((2, 2, channels, tokens), BF16),
            pltpu.VMEM((LINE, pl.cdiv(2 * channels, LANES) * LANES, 2 * tokens), BF16),
            pltpu.VMEM((depth, LANES), F32),
            pltpu.VMEM((rows, 2 * tokens), F32),
            pltpu.VMEM((tokens, rows), F32),
            pltpu.VMEM((tokens, rows), F32),
            pltpu.VMEM((2, tokens, hidden), BF16),
            dma((5,)), dma((4,)), dma((4,)), dma((4,)), dma((8,)), dma((4,)), dma((4,)), dma((8,)),
            dma((1,)), dma((2,)), dma((2,)), dma((2,)), dma((2,)), dma((2,)),
            dma((4,)), dma((8,)), dma((4,)), dma((8,)), dma((8,)), dma((6,)), dma((3,)), dma((1,)), dma((1,)), dma((1,)),
        ],
        compiler_params=pltpu.CompilerParams(
            collective_id=0, has_side_effects=True, vmem_limit_bytes=56 * 2**20),
    )(activations, output_grads.T, channel_scale, weight_codes)
    weight_grads, input_grads = pl.pallas_call(
        weight_kernel,
        out_shape=(
            jax.ShapeDtypeStruct((2 * channels, hidden), F32),
            jax.ShapeDtypeStruct((tokens, hidden), F32),
        ),
        in_specs=[anywhere] * 3,
        out_specs=(anywhere,) * 2,
        scratch_shapes=[
            pltpu.VMEM((4, 2 * channels, tokens), BF16),
            pltpu.VMEM((4 * tokens, hidden), BF16),
            pltpu.VMEM((3, TILE, hidden), F32),
            pltpu.VMEM((tokens, hidden), F32),
            dma((4,)), dma((4,)), dma((2,)), dma((3, PARTS)),
        ],
        compiler_params=pltpu.CompilerParams(vmem_limit_bytes=56 * 2**20),
    )(grads, acts, input_grads)
    return input_grads, weight_grads.T


def per_device_plain(activations, weight_codes, channel_scale, output_grads):
    full_rows = lax.all_gather(output_grads, "tensor", axis=1, tiled=True)
    scaled = (full_rows.astype(F32) * channel_scale).astype(BF16)
    input_grads = lax.dot_general(
        scaled, weight_codes, (((1,), (1,)), ((), ())), preferred_element_type=F32)
    grad_columns = lax.all_to_all(full_rows, "dp", split_axis=1, concat_axis=0, tiled=True)
    weight_grads = lax.dot_general(
        lax.all_gather(activations, "dp", axis=0, tiled=True), grad_columns,
        (((0,), (0,)), ((), ())), preferred_element_type=F32)
    return input_grads, weight_grads


def solution(mesh):
    placed = (P("dp", "tensor"), P("tensor", None), P(), P("dp", "tensor"))
    small = mesh.shape["dp"] == 4 and mesh.shape["tensor"] == 2 * LINE

    return jax.shard_map(
        per_device_kernels if small else per_device_plain,
        mesh=mesh,
        in_specs=placed,
        out_specs=(P("dp", "tensor"), P("tensor", "dp")),
        check_vma=False,
    )
```
